32 devices in a mesh: rep: 8 (over z, x), tp: 4 (over y, core).
Axes of the slice: x: 2, y: 2, z: 4, core: 2. Of those that a mesh axis runs over, the one named last changes fastest.
Arguments:
- queries: bfloat16 [8, 512, 1024], P('rep', None, 'tp'), may hold values from -120 to 120
- keys: bfloat16 [8, 512, 1024], P('rep', None, 'tp'), may hold values from -6 to 6
- values: bfloat16 [8, 512, 1024], P('rep', None, 'tp'), may hold values from -6 to 6
- out_weight: bfloat16 [8, 1024, 7168], P('rep', 'tp'), may hold values from -0.1875 to 0.1875
- cotangent: bfloat16 [8, 512, 7168], P('rep', 'tp'), may hold values from -6 to 6
- local_params: bfloat16 [8, 2, 32, 7168], P('rep', None, 'tp'), may hold values from -6 to 6
- global_params: float32 [2, 32, 7168], P(None, 'tp'), may hold values from -6 to 6
- momentum: float32 [2, 32, 7168], P(None, 'tp'), may hold values from -3 to 3
- frag_index: int32 [1], replicated, may hold values from 0 to 1
Outputs:
- branch_out: bfloat16 [8, 512, 7168], P('rep', 'tp')
- weight_grad: bfloat16 [8, 1024, 7168], P('rep', 'tp')
- query_grad: bfloat16 [8, 512, 1024], P('rep', None, 'tp')
- key_grad: bfloat16 [8, 512, 1024], P('rep', None, 'tp')
- value_grad: bfloat16 [8, 512, 1024], P('rep', None, 'tp')
- new_global: float32 [32, 7168], P('tp')
- new_momentum: float32 [32, 7168], P('tp')
The draws below stay inside these ranges and needn't reach their ends.
All inputs are finite; a program needn't handle non-finite values.
Results may differ from the reference program's by a relative error of at most 0.017.
Values may be sent and summed in bfloat16 or wider, within the bound.
A program may use at most 128 MiB of HBM per device.

```python
import jax
import jax.numpy as jnp
from jax import lax

D = 7168
HD = 128
HEADS_DEV = 2
LEN = 512
SEQS = 1
FRAGS = 2
HEADS = 8
TOKENS = 512
FRAG_ROWS = 32
N_REP = 8
N_TP = 4


def query_key_pair(key):
    shape = (N_REP, TOKENS, HEADS * HD)
    base_query = jnp.clip(jax.random.normal(jax.random.fold_in(key, 11), shape, jnp.float32), -6.0, 6.0)
    base_key = jnp.clip(jax.random.normal(jax.random.fold_in(key, 12), shape, jnp.float32), -6.0, 6.0)
    return (base_query, base_key)


def draw_queries(key, part):
    base_query, base_key = query_key_pair(key)
    return base_query.astype(jnp.bfloat16)


def draw_keys(key, part):
    base_query, base_key = query_key_pair(key)
    return base_key.astype(jnp.bfloat16)


def shard_levels(stream_key, extent, split, low, top_value):
    loudness = 1.0
    for dim, blocks in split:
        draws = jax.random.uniform(jax.random.fold_in(jax.random.fold_in(stream_key, 6), dim), (blocks,), jnp.float32, low / len(split), top_value / len(split))
        loudness = loudness * jnp.repeat(jnp.exp(draws), extent[dim] // blocks).reshape((-1,) + (1,) * (len(extent) - 1 - dim))
    return loudness


def gaussian(own_key, shape, spread, most, pieces=(), dtype=jnp.bfloat16):
    entries = jax.random.normal(own_key, shape, jnp.float32) * spread
    if len(pieces) > 0:
        entries = shard_levels(own_key, shape, pieces, -0.22, 0.18) * entries
    return jnp.clip(entries, min=-most, max=most).astype(dtype)


def setup_inputs(seed: int = 0) -> dict:
    key_list = jax.random.split(jax.random.key(seed), 10)
    queries = draw_queries(jax.random.fold_in(key_list[9], 71), 0)
    keys = draw_keys(jax.random.fold_in(key_list[9], 71), 0)
    values = gaussian(key_list[2], (N_REP, TOKENS, HEADS * HD), 1.0, 6.0, ((0, 8), (2, 4)))
    out_weight = gaussian(key_list[3], (N_REP, HEADS * HD, D), (HEADS * HD) ** -0.5, 0.1875, ((0, 8), (1, 4)))
    cotangent = gaussian(key_list[4], (N_REP, TOKENS, D), 1.0, 6.0, ((0, 8), (1, 4)))
    local_params = gaussian(key_list[5], (N_REP, FRAGS, FRAG_ROWS, D), 1.0, 6.0, ((0, 8), (2, 4)))
    global_params = gaussian(key_list[6], (FRAGS, FRAG_ROWS, D), 1.0, 6.0, ((1, 4),), jnp.float32)
    momentum = gaussian(key_list[7], (FRAGS, FRAG_ROWS, D), 0.5, 3.0, ((1, 4),), jnp.float32)
    frag_index = jax.random.randint(key_list[8], (1,), 0, FRAGS).astype(jnp.int32)
    return dict(queries=queries, keys=keys, values=values, out_weight=out_weight, cotangent=cotangent, local_params=local_params, global_params=global_params, momentum=momentum, frag_index=frag_index)


outer_momentum = 0.9
outer_rate = 0.7


def split_heads(array):
    return array.reshape(SEQS, LEN, HEADS, HD).astype(jnp.float32)


def one_replica(inputs):
    queries, keys, values, out_weight, cotangent = inputs
    scale = HD ** -0.5
    query_heads = split_heads(queries)
    key_heads = split_heads(keys)
    value_heads = split_heads(values)
    scores = jnp.einsum("slhd,smhd->shlm", query_heads, key_heads) * scale
    causal = jnp.arange(LEN)[:, None] >= jnp.arange(LEN)[None, :]
    scores = jnp.where(causal[None, None], scores, -1e30)
    top = jnp.max(scores, axis=-1, keepdims=True)
    weights = jnp.exp(scores - top)
    probs = weights / jnp.sum(weights, axis=-1, keepdims=True)
    probs_half = probs.astype(jnp.bfloat16)
    context = jnp.einsum("shlm,smhd->slhd", probs_half.astype(jnp.float32), value_heads)
    context = context.astype(jnp.bfloat16).reshape(TOKENS, HEADS * HD)
    group_cols = HEADS_DEV * HD
    context_groups = context.reshape(TOKENS, N_TP, group_cols).transpose(1, 0, 2)
    weight_groups = out_weight.reshape(N_TP, group_cols, D)

    def add_group(summed, pair):
        partial_term = jnp.dot(pair[0], pair[1], preferred_element_type=jnp.float32).astype(jnp.bfloat16)
        partial_term = lax.optimization_barrier(partial_term)
        return summed + partial_term.astype(jnp.float32), None

    summed, unused = lax.scan(add_group, jnp.zeros((TOKENS, D), jnp.float32), (context_groups, weight_groups))
    branch_out = summed.astype(jnp.bfloat16)
    weight_grad = jnp.dot(context.T, cotangent, preferred_element_type=jnp.float32).astype(jnp.bfloat16)
    context_grad = jnp.dot(cotangent, out_weight.T, preferred_element_type=jnp.float32).astype(jnp.bfloat16)
    context_heads = split_heads(context_grad)
    probs_grad = jnp.einsum("slhd,smhd->shlm", context_heads, value_heads)
    inner = jnp.sum(probs * probs_grad, axis=-1, keepdims=True)
    score_grad = (probs * (probs_grad - inner) * scale).astype(jnp.bfloat16).astype(jnp.float32)
    query_grad = jnp.einsum("shlm,smhd->slhd", score_grad, key_heads)
    key_grad = jnp.einsum("shlm,slhd->smhd", score_grad, query_heads)
    value_grad = jnp.einsum("shlm,slhd->smhd", probs_half.astype(jnp.float32), context_heads)
    shaped = [g.astype(jnp.bfloat16).reshape(TOKENS, HEADS * HD) for g in (query_grad, key_grad, value_grad)]
    return branch_out, weight_grad, shaped[0], shaped[1], shaped[2]


def reference(queries, keys, values, out_weight, cotangent, local_params, global_params, momentum, frag_index):
    results = lax.map(one_replica, (queries, keys, values, out_weight, cotangent))
    chosen = frag_index[0].astype(jnp.int32)
    local_sel = lax.dynamic_index_in_dim(local_params, chosen, 1, keepdims=False).astype(jnp.float32)
    average = jnp.sum(local_sel, axis=0) / N_REP
    outer_old = lax.dynamic_index_in_dim(global_params, chosen, 0, keepdims=False)
    moment_old = lax.dynamic_index_in_dim(momentum, chosen, 0, keepdims=False)
    pseudo_grad = outer_old - average
    new_momentum = outer_momentum * moment_old + pseudo_grad
    new_global = outer_old - outer_rate * (outer_momentum * new_momentum + pseudo_grad)
    return results[0], results[1], results[2], results[3], results[4], new_global, new_momentum
```

```python
import jax
import jax.numpy as jnp
from jax import lax
from jax.sharding import PartitionSpec as P

HD = 128
LEN = 512
SEQS = 1


outer_momentum = 0.9
outer_rate = 0.7


def nesterov(outer_old, moment_old, summed):
    average = summed / lax.axis_size("rep")
    pseudo_grad = outer_old - average
    new_momentum = outer_momentum * moment_old + pseudo_grad
    new_global = outer_old - outer_rate * (outer_momentum * new_momentum + pseudo_grad)
    return (new_global, new_momentum)


def outer_update(local_params, global_params, momentum, frag_index, after):
    chosen = frag_index[0]
    local_sel = lax.dynamic_index_in_dim(local_params[0], chosen, 0, keepdims=False).astype(
        jnp.float32
    )
    outer_old = lax.dynamic_index_in_dim(global_params, chosen, 0, keepdims=False)
    moment_old = lax.dynamic_index_in_dim(momentum, chosen, 0, keepdims=False)
    summed = lax.psum(local_sel.astype(jnp.bfloat16), "rep")
    summed, after = lax.optimization_barrier((summed, after))
    summed = summed.astype(jnp.float32)
    return nesterov(outer_old, moment_old, summed)


def sibling_pairs(size):
    return [(t, t ^ 1) for t in range(size)]


def chip_shift(size, step):
    chips = size // 2
    return [(t, ((t // 2 + step) % chips) * 2 + t % 2) for t in range(size)]


def rows_of(array, owner, count):
    return lax.dynamic_slice_in_dim(array, owner * count, count, 0)


def inner_step(queries, keys, values, out_weight, cotangent):
    scale = HD ** (-0.5)
    head_cols = queries.shape[2]
    heads_here = head_cols // HD
    tokens = queries.shape[1]
    weight_here = out_weight[0]
    cot_here = cotangent[0]
    own_rows = cot_here.shape[0]
    size = lax.axis_size("tp")
    chips = size // 2
    me = lax.axis_index("tp")
    chip, core = me // 2, me % 2
    pairs = sibling_pairs(size)

    cot_far = [lax.ppermute(cot_here, "tp", chip_shift(size, k)) for k in range(1, chips)]
    cot_near = lax.ppermute(cot_here, "tp", pairs)
    weight_near = lax.ppermute(weight_here, "tp", pairs)

    query_heads = queries[0].reshape(SEQS, LEN, heads_here, HD)
    key_heads = keys[0].reshape(SEQS, LEN, heads_here, HD)
    value_heads = values[0].reshape(SEQS, LEN, heads_here, HD)
    scores = (
        jnp.einsum("slhd,smhd->shlm", query_heads, key_heads, preferred_element_type=jnp.float32)
        * scale
    )
    causal = jnp.arange(LEN)[:, None] >= jnp.arange(LEN)[None, :]
    scores = jnp.where(causal[None, None], scores, -1e30)
    top = jnp.max(scores, axis=-1, keepdims=True)
    weights = jnp.exp(scores - top)
    probs = weights / jnp.sum(weights, axis=-1, keepdims=True)
    probs_half = probs.astype(jnp.bfloat16)
    context = jnp.einsum(
        "shlm,smhd->slhd", probs_half, value_heads, preferred_element_type=jnp.float32
    )
    context = context.astype(jnp.bfloat16).reshape(tokens, head_cols)

    give = jnp.concatenate(
        [rows_of(context, ((chip + k) % chips) * 2 + 1 - core, own_rows) for k in range(chips)]
    )
    taken = lax.ppermute(give, "tp", pairs)
    mine = jnp.concatenate(
        [rows_of(context, ((chip + k) % chips) * 2 + core, own_rows) for k in range(chips)]
    )
    both = jnp.concatenate([mine, taken], axis=1)
    weight_both = jnp.concatenate([weight_here, weight_near], axis=0)
    far = [
        jnp.dot(
            both[k * own_rows : (k + 1) * own_rows], weight_both, preferred_element_type=jnp.float32
        ).astype(jnp.bfloat16)
        for k in range(1, chips)
    ]
    own = jnp.dot(both[:own_rows], weight_both, preferred_element_type=jnp.float32)
    far, cot_far, own = lax.optimization_barrier((far, cot_far, own))
    got = [lax.ppermute(p, "tp", chip_shift(size, k)) for k, p in enumerate(far, 1)]
    for part in got:
        own = own + part.astype(jnp.float32)
    branch_out = own.astype(jnp.bfloat16)

    cot_far_near = [lax.ppermute(c, "tp", pairs) for c in cot_far]
    blocks = [cot_here, cot_near]
    owners = [me, chip * 2 + 1 - core]
    for k in range(1, chips):
        from_chip = (chip - k + chips) % chips
        blocks += [cot_far[k - 1], cot_far_near[k - 1]]
        owners += [from_chip * 2 + core, from_chip * 2 + 1 - core]
    block_rows = jnp.concatenate(blocks)
    context_rows = jnp.concatenate([rows_of(context, o, own_rows) for o in owners])
    weight_grad = lax.dot_general(
        context_rows, block_rows, (((0,), (0,)), ((), ())), preferred_element_type=jnp.float32
    ).astype(jnp.bfloat16)
    part_grad = lax.dot_general(
        block_rows, weight_here, (((1,), (1,)), ((), ())), preferred_element_type=jnp.float32
    ).astype(jnp.bfloat16)
    context_grad = jnp.zeros((tokens, head_cols), jnp.bfloat16)
    for i, o in enumerate(owners):
        context_grad = lax.dynamic_update_slice_in_dim(
            context_grad, part_grad[i * own_rows : (i + 1) * own_rows], o * own_rows, 0
        )
    context_grad = context_grad.reshape(SEQS, LEN, heads_here, HD)
    probs_grad = jnp.einsum(
        "slhd,smhd->shlm", context_grad, value_heads, preferred_element_type=jnp.float32
    )
    inner = jnp.sum(probs * probs_grad, axis=-1, keepdims=True)
    score_grad = (probs * (probs_grad - inner) * scale).astype(jnp.bfloat16)
    query_grad = jnp.einsum(
        "shlm,smhd->slhd", score_grad, key_heads, preferred_element_type=jnp.float32
    )
    key_grad = jnp.einsum(
        "shlm,slhd->smhd", score_grad, query_heads, preferred_element_type=jnp.float32
    )
    value_grad = jnp.einsum(
        "shlm,slhd->smhd", probs_half, context_grad, preferred_element_type=jnp.float32
    )
    shaped = [
        g.astype(jnp.bfloat16).reshape(1, tokens, head_cols)
        for g in (query_grad, key_grad, value_grad)
    ]
    return (branch_out[None], weight_grad[None], shaped[0], shaped[1], shaped[2])


def shards(
    queries, keys, values, out_weight, cotangent, local_params, global_params, momentum, frag_index
):
    results = inner_step(queries, keys, values, out_weight, cotangent)
    new_global, new_momentum = outer_update(
        local_params, global_params, momentum, frag_index, results[2]
    )
    return (results[0], results[1], results[2], results[3], results[4], new_global, new_momentum)


def solution(mesh):
    placed = (
        P("rep", None, "tp"),
        P("rep", None, "tp"),
        P("rep", None, "tp"),
        P("rep", "tp", None),
        P("rep", "tp", None),
        P("rep", None, "tp", None),
        P(None, "tp", None),
        P(None, "tp", None),
        P(),
    )
    return jax.shard_map(
        shards,
        mesh=mesh,
        in_specs=placed,
        out_specs=(
            P("rep", "tp", None),
            P("rep", "tp", None),
            P("rep", None, "tp"),
            P("rep", None, "tp"),
            P("rep", None, "tp"),
            P("tp", None),
            P("tp", None),
        ),
        check_vma=False,
    )
```

```python
import jax
import jax.numpy as jnp
from jax import lax
from jax.experimental import pallas as pl
from jax.experimental.pallas import tpu as pltpu
from jax.sharding import PartitionSpec as P

HD = 128
LEN = 512
SEQS = 1


outer_momentum = 0.9
outer_rate = 0.7


def nesterov(outer_old, moment_old, summed):
    average = summed / lax.axis_size("rep")
    pseudo_grad = outer_old - average
    new_momentum = outer_momentum * moment_old + pseudo_grad
    new_global = outer_old - outer_rate * (outer_momentum * new_momentum + pseudo_grad)
    return (new_global, new_momentum)


def sum_replicas(local_sel):
    size = lax.axis_size("rep")
    others = [
        lax.ppermute(local_sel, "rep", [(r, (r + k) % size) for r in range(size)])
        for k in range(1, size)
    ]
    total = local_sel.astype(jnp.float32)
    for other in others:
        total = total + other.astype(jnp.float32)
    return total


def outer_update(summed, global_params, momentum, frag_index):
    chosen = frag_index[0]
    outer_old = lax.dynamic_index_in_dim(global_params, chosen, 0, keepdims=False)
    moment_old = lax.dynamic_index_in_dim(momentum, chosen, 0, keepdims=False)
    return nesterov(outer_old, moment_old, summed)


def sibling_pairs(size):
    return [(t, t ^ 1) for t in range(size)]


def chip_shift(size, step):
    chips = size // 2
    return [(t, ((t // 2 + step) % chips) * 2 + t % 2) for t in range(size)]


def rows_of(array, owner, count):
    return lax.dynamic_slice_in_dim(array, owner * count, count, 0)


def dot(a, b, over):
    return lax.dot_general(a, b, ((over[:1], over[1:]), ((), ())), preferred_element_type=jnp.float32)


def vmem(mib):
    return pltpu.CompilerParams(vmem_limit_bytes=mib * 2**20)


def cost(flops, *arrays):
    moved = sum(a.size * a.dtype.itemsize for a in arrays)
    return pl.CostEstimate(flops=flops, bytes_accessed=moved, transcendentals=0)


def column_block(cols):
    return 1024 if cols % 1024 == 0 else cols


def softmax_rows(query, key, first):
    scores = dot(query, key, (1, 1)) * HD ** (-0.5)
    row = lax.broadcasted_iota(jnp.int32, scores.shape, 0) + first
    col = lax.broadcasted_iota(jnp.int32, scores.shape, 1)
    scores = jnp.where(row >= col, scores, -1e30)
    weights = jnp.exp(scores - jnp.max(scores, axis=-1, keepdims=True))
    return weights / jnp.sum(weights, axis=-1, keepdims=True)


ROWS = 256


def forward_kernel(q_ref, k_ref, v_ref, out_ref):
    for first in range(0, LEN, ROWS):
        end = first + ROWS
        probs = softmax_rows(q_ref[first:end, :], k_ref[:end, :], first)
        out_ref[first:end, :] = dot(probs.astype(jnp.bfloat16), v_ref[:end, :], (1, 0)).astype(
            jnp.bfloat16
        )


def backward_kernel(q_ref, k_ref, v_ref, g_ref, dq_ref, dk_ref, dv_ref, dk_acc, dv_acc):
    dk_acc[...] = jnp.zeros_like(dk_acc)
    dv_acc[...] = jnp.zeros_like(dv_acc)
    for first in range(0, LEN, ROWS):
        end = first + ROWS
        query, grad = q_ref[first:end, :], g_ref[first:end, :]
        probs = softmax_rows(query, k_ref[:end, :], first)
        probs_grad = dot(grad, v_ref[:end, :], (1, 1))
        inner = jnp.sum(probs * probs_grad, axis=-1, keepdims=True)
        score_grad = (probs * (probs_grad - inner) * HD ** (-0.5)).astype(jnp.bfloat16)
        dq_ref[first:end, :] = dot(score_grad, k_ref[:end, :], (1, 0)).astype(jnp.bfloat16)
        dk_acc[:end, :] += dot(score_grad, query, (0, 0))
        dv_acc[:end, :] += dot(probs.astype(jnp.bfloat16), grad, (0, 0))
    dk_ref[...] = dk_acc[...].astype(jnp.bfloat16)
    dv_ref[...] = dv_acc[...].astype(jnp.bfloat16)


def attention_forward(query, key, value):
    spec = pl.BlockSpec((LEN, HD), lambda h: (0, h))
    return pl.pallas_call(
        forward_kernel,
        grid=(query.shape[1] // HD,),
        in_specs=[spec] * 3,
        out_specs=spec,
        out_shape=jax.ShapeDtypeStruct(query.shape, jnp.bfloat16),
        compiler_params=vmem(32),
    )(query, key, value)


def attention_backward(query, key, value, grad):
    spec = pl.BlockSpec((LEN, HD), lambda h: (0, h))
    return pl.pallas_call(
        backward_kernel,
        grid=(query.shape[1] // HD,),
        in_specs=[spec] * 4,
        out_specs=[spec] * 3,
        out_shape=[jax.ShapeDtypeStruct(query.shape, jnp.bfloat16)] * 3,
        scratch_shapes=[pltpu.VMEM((LEN, HD), jnp.float32)] * 2,
        compiler_params=vmem(32),
        cost_estimate=cost(10 * LEN * query.size, query, key, value, grad, query, key, value),
    )(query, key, value, grad)


def branch_kernel(mine_ref, taken_ref, here_ref, near_ref, *out_refs):
    total = dot(mine_ref[...], here_ref[...], (1, 0)) + dot(taken_ref[...], near_ref[...], (1, 0))
    rows = out_refs[0].shape[0]
    for k, out in enumerate(out_refs):
        out[...] = total[k * rows : (k + 1) * rows].astype(out.dtype)


def branch_parts(mine, taken, here, near, chips):
    rows, cols = mine.shape[0] // chips, here.shape[1]
    block = column_block(cols)
    whole = pl.BlockSpec(mine.shape, lambda i: (0, 0))
    weight = pl.BlockSpec((here.shape[0], block), lambda i: (0, i))
    out = jax.ShapeDtypeStruct((rows, cols), jnp.bfloat16)
    return pl.pallas_call(
        branch_kernel,
        grid=(cols // block,),
        in_specs=[whole, whole, weight, weight],
        out_specs=[pl.BlockSpec((rows, block), lambda i: (0, i))] * chips,
        out_shape=[out] * chips,
        compiler_params=vmem(32),
    )(mine, taken, here, near)


def grads_kernel(*refs):
    context_ref, weight_ref, *cot_refs = refs[:-3]
    wgrad_ref, cgrad_ref, total = refs[-3:]
    step = pl.program_id(0)

    @pl.when(step == 0)
    def _():
        total[...] = jnp.zeros_like(total)

    cot = jnp.concatenate([c[...] for c in cot_refs], axis=0)
    wgrad_ref[...] = dot(context_ref[...], cot, (1, 0)).astype(wgrad_ref.dtype)
    total[...] += dot(cot, weight_ref[...], (1, 1))

    @pl.when(step == pl.num_programs(0) - 1)
    def _():
        cgrad_ref[...] = total[...].astype(cgrad_ref.dtype)


def projection_grads(context_t, weight, cots):
    features, tokens = context_t.shape
    rows, cols = cots[0].shape
    block = column_block(cols)
    column = pl.BlockSpec((features, block), lambda i: (0, i))
    out = [
        jax.ShapeDtypeStruct((features, cols), jnp.bfloat16),
        jax.ShapeDtypeStruct((tokens, features), jnp.bfloat16),
    ]
    return pl.pallas_call(
        grads_kernel,
        grid=(cols // block,),
        in_specs=[pl.BlockSpec((features, tokens), lambda i: (0, 0)), column]
        + [pl.BlockSpec((rows, block), lambda i: (0, i))] * len(cots),
        out_specs=[column, pl.BlockSpec((tokens, features), lambda i: (0, 0))],
        out_shape=out,
        scratch_shapes=[pltpu.VMEM((tokens, features), jnp.float32)],
        compiler_params=vmem(32),
        cost_estimate=cost(4 * tokens * features * cols, context_t, weight, *cots, *out),
    )(context_t, weight, *cots)


def add_kernel(*refs):
    total = refs[0][...].astype(jnp.float32)
    for part in refs[1:-1]:
        total = total + part[...].astype(jnp.float32)
    refs[-1][...] = total.astype(refs[-1].dtype)


def add_parts(parts):
    rows, cols = parts[0].shape
    block = column_block(cols)
    spec = pl.BlockSpec((rows, block), lambda i: (0, i))
    return pl.pallas_call(
        add_kernel,
        grid=(cols // block,),
        in_specs=[spec] * len(parts),
        out_specs=spec,
        out_shape=jax.ShapeDtypeStruct((rows, cols), jnp.bfloat16),
    )(*parts)


def inner_step(queries, keys, values, out_weight, cotangent, local_sel):
    weight_here = out_weight[0]
    cot_here = cotangent[0]
    own_rows = cot_here.shape[0]
    size = lax.axis_size("tp")
    chips = size // 2
    me = lax.axis_index("tp")
    chip, core = me // 2, me % 2
    pairs = sibling_pairs(size)

    cot_far = [lax.ppermute(cot_here, "tp", chip_shift(size, k)) for k in range(1, chips)]
    cot_near = lax.ppermute(cot_here, "tp", pairs)
    weight_near = lax.ppermute(weight_here, "tp", pairs)

    context = attention_forward(queries[0], keys[0], values[0])
    summed = sum_replicas(local_sel)

    give = jnp.concatenate(
        [rows_of(context, ((chip + k) % chips) * 2 + 1 - core, own_rows) for k in range(chips)]
    )
    taken = lax.ppermute(give, "tp", pairs)
    mine = jnp.concatenate(
        [rows_of(context, ((chip + k) % chips) * 2 + core, own_rows) for k in range(chips)]
    )
    own, *far = branch_parts(mine, taken, weight_here, weight_near, chips)
    far, cot_far, own, summed = lax.optimization_barrier((far, cot_far, own, summed))
    got = [lax.ppermute(p, "tp", chip_shift(size, k)) for k, p in enumerate(far, 1)]

    cot_far_near = [lax.ppermute(c, "tp", pairs) for c in cot_far]
    blocks = [cot_here, cot_near]
    owners = [me, chip * 2 + 1 - core]
    for k in range(1, chips):
        from_chip = (chip - k + chips) % chips
        blocks += [cot_far[k - 1], cot_far_near[k - 1]]
        owners += [from_chip * 2 + core, from_chip * 2 + 1 - core]
    context_rows = jnp.concatenate([rows_of(context, o, own_rows) for o in owners])
    weight_grad, part_grad = projection_grads(context_rows.T, weight_here, blocks)
    context_grad = jnp.zeros_like(context)
    for i, o in enumerate(owners):
        context_grad = lax.dynamic_update_slice_in_dim(
            context_grad, part_grad[i * own_rows : (i + 1) * own_rows], o * own_rows, 0
        )
    shaped = attention_backward(queries[0], keys[0], values[0], context_grad)
    got, weight_grad, shaped = lax.optimization_barrier((got, weight_grad, shaped))
    branch_out = add_parts([own] + got)
    return (branch_out[None], weight_grad[None], *[g[None] for g in shaped], summed)


def shards(
    queries, keys, values, out_weight, cotangent, local_params, global_params, momentum, frag_index
):
    local_sel = lax.dynamic_index_in_dim(local_params[0], frag_index[0], 0, keepdims=False)
    *results, summed = inner_step(queries, keys, values, out_weight, cotangent, local_sel)
    new_global, new_momentum = outer_update(summed, global_params, momentum, frag_index)
    return (results[0], results[1], results[2], results[3], results[4], new_global, new_momentum)


def solution(mesh):
    placed = (
        P("rep", None, "tp"),
        P("rep", None, "tp"),
        P("rep", None, "tp"),
        P("rep", "tp", None),
        P("rep", "tp", None),
        P("rep", None, "tp", None),
        P(None, "tp", None),
        P(None, "tp", None),
        P(),
    )
    return jax.shard_map(
        shards,
        mesh=mesh,
        in_specs=placed,
        out_specs=(
            P("rep", "tp", None),
            P("rep", "tp", None),
            P("rep", None, "tp"),
            P("rep", None, "tp"),
            P("rep", None, "tp"),
            P("tp", None),
            P("tp", None),
        ),
        check_vma=False,
    )
```

```python
import jax
import jax.numpy as jnp
from jax import lax
from jax.experimental import pallas as pl
from jax.experimental.pallas import tpu as pltpu
from jax.sharding import PartitionSpec as P

HD = 128
LEN = 512
SEQS = 1


outer_momentum = 0.9
outer_rate = 0.7


def nesterov(outer_old, moment_old, summed):
    average = summed / lax.axis_size("rep")
    pseudo_grad = outer_old - average
    new_momentum = outer_momentum * moment_old + pseudo_grad
    new_global = outer_old - outer_rate * (outer_momentum * new_momentum + pseudo_grad)
    return (new_global, new_momentum)


def swap_add(total, step):
    size = lax.axis_size("rep")
    other = lax.ppermute(total, "rep", [(r, r ^ step) for r in range(size)])
    return total.astype(jnp.float32) + other.astype(jnp.float32)


def sum_steps():
    size = lax.axis_size("rep")
    if size & (size - 1):
        raise ValueError("rep")
    return [1 << i for i in range(size.bit_length() - 1)]


def outer_update(summed, global_params, momentum, frag_index):
    chosen = frag_index[0]
    outer_old = lax.dynamic_index_in_dim(global_params, chosen, 0, keepdims=False)
    moment_old = lax.dynamic_index_in_dim(momentum, chosen, 0, keepdims=False)
    return nesterov(outer_old, moment_old, summed)


def sibling_pairs(size):
    return [(t, t ^ 1) for t in range(size)]


def chip_shift(size, step):
    chips = size // 2
    return [(t, ((t // 2 + step) % chips) * 2 + t % 2) for t in range(size)]


def rows_of(array, owner, count):
    return lax.dynamic_slice_in_dim(array, owner * count, count, 0)


def dot(a, b, over):
    return lax.dot_general(a, b, ((over[:1], over[1:]), ((), ())), preferred_element_type=jnp.float32)


def vmem(mib):
    return pltpu.CompilerParams(vmem_limit_bytes=mib * 2**20)


def cost(flops, *arrays):
    moved = sum(a.size * a.dtype.itemsize for a in arrays)
    return pl.CostEstimate(flops=flops, bytes_accessed=moved, transcendentals=0)


def column_block(cols):
    return 1024 if cols % 1024 == 0 else cols


def softmax_rows(query, key, first):
    scores = dot(query, key, (1, 1)) * HD ** (-0.5)
    row = lax.broadcasted_iota(jnp.int32, scores.shape, 0) + first
    col = lax.broadcasted_iota(jnp.int32, scores.shape, 1)
    scores = jnp.where(row >= col, scores, -1e30)
    weights = jnp.exp(scores - jnp.max(scores, axis=-1, keepdims=True))
    return weights / jnp.sum(weights, axis=-1, keepdims=True)


ROWS = 256


def forward_kernel(q_ref, k_ref, v_ref, out_ref):
    for first in range(0, LEN, ROWS):
        end = first + ROWS
        probs = softmax_rows(q_ref[first:end, :], k_ref[:end, :], first)
        out_ref[first:end, :] = dot(probs.astype(jnp.bfloat16), v_ref[:end, :], (1, 0)).astype(
            jnp.bfloat16
        )


def backward_kernel(q_ref, k_ref, v_ref, g_ref, dq_ref, dk_ref, dv_ref, dk_acc, dv_acc):
    dk_acc[...] = jnp.zeros_like(dk_acc)
    dv_acc[...] = jnp.zeros_like(dv_acc)
    for first in range(0, LEN, ROWS):
        end = first + ROWS
        query, grad = q_ref[first:end, :], g_ref[first:end, :]
        probs = softmax_rows(query, k_ref[:end, :], first)
        probs_grad = dot(grad, v_ref[:end, :], (1, 1))
        inner = jnp.sum(probs * probs_grad, axis=-1, keepdims=True)
        score_grad = (probs * (probs_grad - inner) * HD ** (-0.5)).astype(jnp.bfloat16)
        dq_ref[first:end, :] = dot(score_grad, k_ref[:end, :], (1, 0)).astype(jnp.bfloat16)
        dk_acc[:end, :] += dot(score_grad, query, (0, 0))
        dv_acc[:end, :] += dot(probs.astype(jnp.bfloat16), grad, (0, 0))
    dk_ref[...] = dk_acc[...].astype(jnp.bfloat16)
    dv_ref[...] = dv_acc[...].astype(jnp.bfloat16)


def attention_forward(query, key, value):
    spec = pl.BlockSpec((LEN, HD), lambda h: (0, h))
    return pl.pallas_call(
        forward_kernel,
        grid=(query.shape[1] // HD,),
        in_specs=[spec] * 3,
        out_specs=spec,
        out_shape=jax.ShapeDtypeStruct(query.shape, jnp.bfloat16),
        compiler_params=vmem(32),
    )(query, key, value)


def attention_backward(query, key, value, grad):
    spec = pl.BlockSpec((LEN, HD), lambda h: (0, h))
    return pl.pallas_call(
        backward_kernel,
        grid=(query.shape[1] // HD,),
        in_specs=[spec] * 4,
        out_specs=[spec] * 3,
        out_shape=[jax.ShapeDtypeStruct(query.shape, jnp.bfloat16)] * 3,
        scratch_shapes=[pltpu.VMEM((LEN, HD), jnp.float32)] * 2,
        compiler_params=vmem(32),
        cost_estimate=cost(10 * LEN * query.size, query, key, value, grad, query, key, value),
    )(query, key, value, grad)


def branch_kernel(mine_ref, taken_ref, here_ref, near_ref, *out_refs):
    total = dot(mine_ref[...], here_ref[...], (1, 0)) + dot(taken_ref[...], near_ref[...], (1, 0))
    rows = out_refs[0].shape[0]
    for k, out in enumerate(out_refs):
        out[...] = total[k * rows : (k + 1) * rows].astype(out.dtype)


def branch_parts(mine, taken, here, near, chips):
    rows, cols = mine.shape[0] // chips, here.shape[1]
    block = column_block(cols)
    whole = pl.BlockSpec(mine.shape, lambda i: (0, 0))
    weight = pl.BlockSpec((here.shape[0], block), lambda i: (0, i))
    out = jax.ShapeDtypeStruct((rows, cols), jnp.bfloat16)
    return pl.pallas_call(
        branch_kernel,
        grid=(cols // block,),
        in_specs=[whole, whole, weight, weight],
        out_specs=[pl.BlockSpec((rows, block), lambda i: (0, i))] * chips,
        out_shape=[out] * chips,
        compiler_params=vmem(32),
    )(mine, taken, here, near)


def grads_kernel(*refs):
    context_ref, weight_ref, *cot_refs = refs[:-3]
    wgrad_ref, cgrad_ref, total = refs[-3:]
    step = pl.program_id(0)

    @pl.when(step == 0)
    def _():
        total[...] = jnp.zeros_like(total)

    cot = jnp.concatenate([c[...] for c in cot_refs], axis=0)
    wgrad_ref[...] = dot(context_ref[...], cot, (1, 0)).astype(wgrad_ref.dtype)
    total[...] += dot(cot, weight_ref[...], (1, 1))

    @pl.when(step == pl.num_programs(0) - 1)
    def _():
        cgrad_ref[...] = total[...].astype(cgrad_ref.dtype)


def projection_grads(context_t, weight, cots):
    features, tokens = context_t.shape
    rows, cols = cots[0].shape
    block = column_block(cols)
    column = pl.BlockSpec((features, block), lambda i: (0, i))
    out = [
        jax.ShapeDtypeStruct((features, cols), jnp.bfloat16),
        jax.ShapeDtypeStruct((tokens, features), jnp.bfloat16),
    ]
    return pl.pallas_call(
        grads_kernel,
        grid=(cols // block,),
        in_specs=[pl.BlockSpec((features, tokens), lambda i: (0, 0)), column]
        + [pl.BlockSpec((rows, block), lambda i: (0, i))] * len(cots),
        out_specs=[column, pl.BlockSpec((tokens, features), lambda i: (0, 0))],
        out_shape=out,
        scratch_shapes=[pltpu.VMEM((tokens, features), jnp.float32)],
        compiler_params=vmem(32),
        cost_estimate=cost(4 * tokens * features * cols, context_t, weight, *cots, *out),
    )(context_t, weight, *cots)


def add_kernel(*refs):
    count = (len(refs) - 4) // 2
    parts, out = refs[:count], refs[count]
    held, total, in_sems, out_sems = refs[count + 1 : 2 * count + 1], *refs[2 * count + 1 :]
    rows, chunks = out.shape[0], out_sems.shape[0]
    each = rows // chunks
    reads = [
        [
            pltpu.make_async_copy(
                part.at[pl.ds(c * each, each)], slot.at[pl.ds(c * each, each)], in_sems.at[c, i]
            )
            for i, (part, slot) in enumerate(zip(parts, held))
        ]
        for c in range(chunks)
    ]
    writes = [
        pltpu.make_async_copy(
            total.at[pl.ds(c * each, each)], out.at[pl.ds(c * each, each)], out_sems.at[c]
        )
        for c in range(chunks)
    ]
    for chunk in reads:
        for read in chunk:
            read.start()
    for c in range(chunks):
        for read in reads[c]:
            read.wait()
        here = slice(c * each, (c + 1) * each)
        summed = held[0][here, :].astype(jnp.float32)
        for slot in held[1:]:
            summed = summed + slot[here, :].astype(jnp.float32)
        total[here, :] = summed.astype(total.dtype)
        writes[c].start()
    for write in writes:
        write.wait()


def add_parts(parts):
    rows, cols = parts[0].shape
    chunks = max(1, min(4, rows // 16))
    slot = pltpu.VMEM((rows, cols), jnp.bfloat16)
    anywhere = pl.BlockSpec(memory_space=pl.ANY)
    return pl.pallas_call(
        add_kernel,
        in_specs=[anywhere] * len(parts),
        out_specs=anywhere,
        out_shape=jax.ShapeDtypeStruct((rows, cols), jnp.bfloat16),
        scratch_shapes=[slot] * (len(parts) + 1)
        + [pltpu.SemaphoreType.DMA((chunks, len(parts))), pltpu.SemaphoreType.DMA((chunks,))],
        compiler_params=vmem(24),
    )(*parts)


def inner_step(queries, keys, values, out_weight, cotangent, local_sel, finish):
    weight_here = out_weight[0]
    cot_here = cotangent[0]
    own_rows = cot_here.shape[0]
    size = lax.axis_size("tp")
    chips = size // 2
    me = lax.axis_index("tp")
    chip, core = me // 2, me % 2
    pairs = sibling_pairs(size)

    cot_far = [lax.ppermute(cot_here, "tp", chip_shift(size, k)) for k in range(1, chips)]
    cot_near = lax.ppermute(cot_here, "tp", pairs)
    weight_near = lax.ppermute(weight_here, "tp", pairs)

    context = attention_forward(queries[0], keys[0], values[0])
    summed = local_sel
    for bit in sum_steps()[:1]:
        summed = swap_add(summed, bit)

    give = jnp.concatenate(
        [rows_of(context, ((chip + k) % chips) * 2 + 1 - core, own_rows) for k in range(chips)]
    )
    taken = lax.ppermute(give, "tp", pairs)
    mine = jnp.concatenate(
        [rows_of(context, ((chip + k) % chips) * 2 + core, own_rows) for k in range(chips)]
    )
    own, *far = branch_parts(mine, taken, weight_here, weight_near, chips)
    far, cot_far, own, summed = lax.optimization_barrier((far, cot_far, own, summed))
    got = [lax.ppermute(p, "tp", chip_shift(size, k)) for k, p in enumerate(far, 1)]

    cot_far_near = [lax.ppermute(c, "tp", pairs) for c in cot_far]
    blocks = [cot_here, cot_near]
    owners = [me, chip * 2 + 1 - core]
    for k in range(1, chips):
        from_chip = (chip - k + chips) % chips
        blocks += [cot_far[k - 1], cot_far_near[k - 1]]
        owners += [from_chip * 2 + core, from_chip * 2 + 1 - core]
    context_rows = jnp.concatenate([rows_of(context, o, own_rows) for o in owners])
    weight_grad, part_grad = projection_grads(context_rows.T, weight_here, blocks)
    part_grad, summed = lax.optimization_barrier((part_grad, summed))
    for bit in sum_steps()[1:]:
        summed = swap_add(summed, bit)
    context_grad = jnp.zeros_like(context)
    for i, o in enumerate(owners):
        context_grad = lax.dynamic_update_slice_in_dim(
            context_grad, part_grad[i * own_rows : (i + 1) * own_rows], o * own_rows, 0
        )
    shaped = attention_backward(queries[0], keys[0], values[0], context_grad)
    outer = finish(summed)
    got, weight_grad, shaped, outer = lax.optimization_barrier((got, weight_grad, shaped, outer))
    branch_out = add_parts([own] + got)
    return (branch_out[None], weight_grad[None], *[g[None] for g in shaped], *outer)


def shards(
    queries, keys, values, out_weight, cotangent, local_params, global_params, momentum, frag_index
):
    local_sel = lax.dynamic_index_in_dim(local_params[0], frag_index[0], 0, keepdims=False)

    def finish(summed):
        return outer_update(summed, global_params, momentum, frag_index)

    return inner_step(queries, keys, values, out_weight, cotangent, local_sel, finish)


def solution(mesh):
    placed = (
        P("rep", None, "tp"),
        P("rep", None, "tp"),
        P("rep", None, "tp"),
        P("rep", "tp", None),
        P("rep", "tp", None),
        P("rep", None, "tp", None),
        P(None, "tp", None),
        P(None, "tp", None),
        P(),
    )
    return jax.shard_map(
        shards,
        mesh=mesh,
        in_specs=placed,
        out_specs=(
            P("rep", "tp", None),
            P("rep", "tp", None),
            P("rep", None, "tp"),
            P("rep", None, "tp"),
            P("rep", None, "tp"),
            P("tp", None),
            P("tp", None),
        ),
        check_vma=False,
    )
```

```python
import functools

import jax
import jax.numpy as jnp
from jax import lax
from jax.experimental import pallas as pl
from jax.experimental.pallas import tpu as pltpu
from jax.sharding import PartitionSpec as P

HD = 128
LEN = 512
SEQS = 1


outer_momentum = 0.9
outer_rate = 0.7


def nesterov(outer_old, moment_old, summed):
    average = summed / lax.axis_size("rep")
    pseudo_grad = outer_old - average
    new_momentum = outer_momentum * moment_old + pseudo_grad
    new_global = outer_old - outer_rate * (outer_momentum * new_momentum + pseudo_grad)
    return (new_global, new_momentum)


def swap_add(total, step):
    size = lax.axis_size("rep")
    other = lax.ppermute(total, "rep", [(r, r ^ step) for r in range(size)])
    return total.astype(jnp.float32) + other.astype(jnp.float32)


def sum_steps():
    size = lax.axis_size("rep")
    if size & (size - 1):
        raise ValueError("rep")
    return [1 << i for i in range(size.bit_length() - 1)]


def outer_update(summed, global_params, momentum, frag_index):
    chosen = frag_index[0]
    outer_old = lax.dynamic_index_in_dim(global_params, chosen, 0, keepdims=False)
    moment_old = lax.dynamic_index_in_dim(momentum, chosen, 0, keepdims=False)
    return nesterov(outer_old, moment_old, summed)


def sibling_pairs(size):
    return [(t, t ^ 1) for t in range(size)]


def chip_shift(size, step):
    chips = size // 2
    return [(t, ((t // 2 + step) % chips) * 2 + t % 2) for t in range(size)]


def rows_of(array, owner, count):
    return lax.dynamic_slice_in_dim(array, owner * count, count, 0)


def dot(a, b, over):
    return lax.dot_general(a, b, ((over[:1], over[1:]), ((), ())), preferred_element_type=jnp.float32)


def vmem(mib):
    return pltpu.CompilerParams(vmem_limit_bytes=mib * 2**20)


def cost(flops, *arrays):
    moved = sum(a.size * a.dtype.itemsize for a in arrays)
    return pl.CostEstimate(flops=flops, bytes_accessed=moved, transcendentals=0)


def column_block(cols):
    return 1024 if cols % 1024 == 0 else cols


def softmax_rows(query, key, first):
    scores = dot(query, key, (1, 1)) * HD ** (-0.5)
    row = lax.broadcasted_iota(jnp.int32, scores.shape, 0) + first
    col = lax.broadcasted_iota(jnp.int32, scores.shape, 1)
    scores = jnp.where(row >= col, scores, -1e30)
    weights = jnp.exp(scores - jnp.max(scores, axis=-1, keepdims=True))
    return weights / jnp.sum(weights, axis=-1, keepdims=True)


ROWS = 256


def forward_kernel(q_ref, k_ref, v_ref, out_ref):
    for first in range(0, LEN, ROWS):
        end = first + ROWS
        probs = softmax_rows(q_ref[first:end, :], k_ref[:end, :], first)
        out_ref[first:end, :] = dot(probs.astype(jnp.bfloat16), v_ref[:end, :], (1, 0)).astype(
            jnp.bfloat16
        )


def backward_kernel(q_ref, k_ref, v_ref, g_ref, dq_ref, dk_ref, dv_ref, dk_acc, dv_acc):
    dk_acc[...] = jnp.zeros_like(dk_acc)
    dv_acc[...] = jnp.zeros_like(dv_acc)
    for first in range(0, LEN, ROWS):
        end = first + ROWS
        query, grad = q_ref[first:end, :], g_ref[first:end, :]
        probs = softmax_rows(query, k_ref[:end, :], first)
        probs_grad = dot(grad, v_ref[:end, :], (1, 1))
        inner = jnp.sum(probs * probs_grad, axis=-1, keepdims=True)
        score_grad = (probs * (probs_grad - inner) * HD ** (-0.5)).astype(jnp.bfloat16)
        dq_ref[first:end, :] = dot(score_grad, k_ref[:end, :], (1, 0)).astype(jnp.bfloat16)
        dk_acc[:end, :] += dot(score_grad, query, (0, 0))
        dv_acc[:end, :] += dot(probs.astype(jnp.bfloat16), grad, (0, 0))
    dk_ref[...] = dk_acc[...].astype(jnp.bfloat16)
    dv_ref[...] = dv_acc[...].astype(jnp.bfloat16)


def attention_forward(query, key, value):
    spec = pl.BlockSpec((LEN, HD), lambda h: (0, h))
    return pl.pallas_call(
        forward_kernel,
        grid=(query.shape[1] // HD,),
        in_specs=[spec] * 3,
        out_specs=spec,
        out_shape=jax.ShapeDtypeStruct(query.shape, jnp.bfloat16),
        compiler_params=vmem(32),
    )(query, key, value)


def attention_backward(query, key, value, grad):
    spec = pl.BlockSpec((LEN, HD), lambda h: (0, h))
    return pl.pallas_call(
        backward_kernel,
        grid=(query.shape[1] // HD,),
        in_specs=[spec] * 4,
        out_specs=[spec] * 3,
        out_shape=[jax.ShapeDtypeStruct(query.shape, jnp.bfloat16)] * 3,
        scratch_shapes=[pltpu.VMEM((LEN, HD), jnp.float32)] * 2,
        compiler_params=vmem(32),
        cost_estimate=cost(10 * LEN * query.size, query, key, value, grad, query, key, value),
    )(query, key, value, grad)


def row_pieces(rows):
    half, quarter = rows // 2, rows // 4
    if quarter % 16 == 0:
        return [(0, quarter), (quarter, half), (half, rows)]
    return [(0, half), (half, rows)]


def branch_kernel(mine_ref, taken_ref, here_ref, near_ref, *out_refs):
    total = dot(mine_ref[...], here_ref[...], (1, 0)) + dot(taken_ref[...], near_ref[...], (1, 0))
    first = 0
    for out in out_refs:
        rows = out.shape[0]
        out[...] = total[first : first + rows].astype(out.dtype)
        first += rows


def branch_parts(mine, taken, here, near, chips):
    rows, cols = mine.shape[0] // chips, here.shape[1]
    pieces = [end - first for first, end in row_pieces(rows)]
    block = column_block(cols)
    whole = pl.BlockSpec(mine.shape, lambda i: (0, 0))
    weight = pl.BlockSpec((here.shape[0], block), lambda i: (0, i))
    outs = pl.pallas_call(
        branch_kernel,
        grid=(cols // block,),
        in_specs=[whole, whole, weight, weight],
        out_specs=[pl.BlockSpec((r, block), lambda i: (0, i)) for r in pieces] * chips,
        out_shape=[jax.ShapeDtypeStruct((r, cols), jnp.bfloat16) for r in pieces] * chips,
        compiler_params=vmem(32),
    )(mine, taken, here, near)
    count = len(pieces)
    return [outs[k * count : (k + 1) * count] for k in range(chips)]


def grads_kernel(*refs):
    context_ref, weight_ref, *cot_refs = refs[:-3]
    wgrad_ref, cgrad_ref, total = refs[-3:]
    step = pl.program_id(0)

    @pl.when(step == 0)
    def _():
        total[...] = jnp.zeros_like(total)

    cot = jnp.concatenate([c[...] for c in cot_refs], axis=0)
    wgrad_ref[...] = dot(context_ref[...], cot, (1, 0)).astype(wgrad_ref.dtype)
    total[...] += dot(cot, weight_ref[...], (1, 1))

    @pl.when(step == pl.num_programs(0) - 1)
    def _():
        cgrad_ref[...] = total[...].astype(cgrad_ref.dtype)


def projection_grads(context_t, weight, cots):
    features, tokens = context_t.shape
    rows, cols = cots[0].shape
    block = column_block(cols)
    column = pl.BlockSpec((features, block), lambda i: (0, i))
    out = [
        jax.ShapeDtypeStruct((features, cols), jnp.bfloat16),
        jax.ShapeDtypeStruct((tokens, features), jnp.bfloat16),
    ]
    return pl.pallas_call(
        grads_kernel,
        grid=(cols // block,),
        in_specs=[pl.BlockSpec((features, tokens), lambda i: (0, 0)), column]
        + [pl.BlockSpec((rows, block), lambda i: (0, i))] * len(cots),
        out_specs=[column, pl.BlockSpec((tokens, features), lambda i: (0, 0))],
        out_shape=out,
        scratch_shapes=[pltpu.VMEM((tokens, features), jnp.float32)],
        compiler_params=vmem(32),
        cost_estimate=cost(4 * tokens * features * cols, context_t, weight, *cots, *out),
    )(context_t, weight, *cots)


CHUNK = 16


def add_kernel(groups, inputs, *refs):
    arrays, out, scratch = refs[:inputs], refs[inputs], list(refs[inputs + 1 :])
    in_sems, out_sems = scratch[-2:]
    work, taken, done = [], 0, 0
    for first, rows, count in groups:
        parts, slots = arrays[taken : taken + count], scratch[taken : taken + count]
        total = scratch[sum(g[2] for g in groups) + groups.index((first, rows, count))]
        taken += count
        for c in range(rows // CHUNK):
            here = pl.ds(c * CHUNK, CHUNK)
            reads = [
                pltpu.make_async_copy(part.at[here], slot.at[here], in_sems.at[done, i])
                for i, (part, slot) in enumerate(zip(parts, slots))
            ]
            there = pl.ds(first + c * CHUNK, CHUNK)
            write = pltpu.make_async_copy(total.at[here], out.at[there], out_sems.at[done])
            work.append((here, slots, total, reads, write))
            done += 1
    for _, _, _, reads, _ in work:
        for read in reads:
            read.start()
    for here, slots, total, reads, write in work:
        for read in reads:
            read.wait()
        summed = slots[0][here, :].astype(jnp.float32)
        for slot in slots[1:]:
            summed = summed + slot[here, :].astype(jnp.float32)
        total[here, :] = summed.astype(total.dtype)
        write.start()
    for _, _, _, _, write in work:
        write.wait()


def add_parts(groups, rows, base=None):
    cols = groups[0][1][0].shape[1]
    arrays = [part for _, parts in groups for part in parts]
    shapes = [(first, parts[0].shape[0], len(parts)) for first, parts in groups]
    chunks = sum(r // CHUNK for _, r, _ in shapes)
    slots = [pltpu.VMEM(a.shape, jnp.bfloat16) for a in arrays]
    slots += [pltpu.VMEM((r, cols), jnp.bfloat16) for _, r, _ in shapes]
    inputs = arrays if base is None else arrays + [base]
    anywhere = pl.BlockSpec(memory_space=pl.ANY)
    return pl.pallas_call(
        functools.partial(add_kernel, shapes, len(inputs)),
        in_specs=[anywhere] * len(inputs),
        out_specs=anywhere,
        out_shape=jax.ShapeDtypeStruct((rows, cols), jnp.bfloat16),
        scratch_shapes=slots
        + [
            pltpu.SemaphoreType.DMA((chunks, max(n for _, _, n in shapes))),
            pltpu.SemaphoreType.DMA((chunks,)),
        ],
        input_output_aliases={} if base is None else {len(arrays): 0},
        compiler_params=vmem(24),
    )(*inputs)


def inner_step(queries, keys, values, out_weight, cotangent, local_sel, finish):
    weight_here = out_weight[0]
    cot_here = cotangent[0]
    own_rows = cot_here.shape[0]
    size = lax.axis_size("tp")
    chips = size // 2
    me = lax.axis_index("tp")
    chip, core = me // 2, me % 2
    pairs = sibling_pairs(size)

    cot_far = [lax.ppermute(cot_here, "tp", chip_shift(size, k)) for k in range(1, chips)]
    cot_near = lax.ppermute(cot_here, "tp", pairs)
    weight_near = lax.ppermute(weight_here, "tp", pairs)

    context = attention_forward(queries[0], keys[0], values[0])
    summed = local_sel
    for bit in sum_steps()[:1]:
        summed = swap_add(summed, bit)

    give = jnp.concatenate(
        [rows_of(context, ((chip + k) % chips) * 2 + 1 - core, own_rows) for k in range(chips)]
    )
    taken = lax.ppermute(give, "tp", pairs)
    mine = jnp.concatenate(
        [rows_of(context, ((chip + k) % chips) * 2 + core, own_rows) for k in range(chips)]
    )
    own, *far = branch_parts(mine, taken, weight_here, weight_near, chips)
    bounds = row_pieces(own_rows)
    own, far, cot_far, summed = lax.optimization_barrier((own, far, cot_far, summed))
    got = [
        [lax.ppermute(p, "tp", chip_shift(size, k)) for p in pieces]
        for k, pieces in enumerate(far, 1)
    ]

    cot_far_near = [lax.ppermute(c, "tp", pairs) for c in cot_far]
    blocks = [cot_here, cot_near]
    owners = [me, chip * 2 + 1 - core]
    for k in range(1, chips):
        from_chip = (chip - k + chips) % chips
        blocks += [cot_far[k - 1], cot_far_near[k - 1]]
        owners += [from_chip * 2 + core, from_chip * 2 + 1 - core]
    context_rows = jnp.concatenate([rows_of(context, o, own_rows) for o in owners])
    weight_grad, part_grad = projection_grads(context_rows.T, weight_here, blocks)
    part_grad, summed = lax.optimization_barrier((part_grad, summed))
    for bit in sum_steps()[1:]:
        summed = swap_add(summed, bit)
    context_grad = jnp.zeros_like(context)
    for i, o in enumerate(owners):
        context_grad = lax.dynamic_update_slice_in_dim(
            context_grad, part_grad[i * own_rows : (i + 1) * own_rows], o * own_rows, 0
        )
    shaped = attention_backward(queries[0], keys[0], values[0], context_grad)
    groups = [
        (first, [own[i]] + [g[i] for g in got]) for i, (first, _) in enumerate(bounds)
    ]
    outer = finish(summed)
    first_groups, shaped = lax.optimization_barrier((groups[:-1], shaped))
    early = add_parts([(bounds[i][0], g[1]) for i, g in enumerate(first_groups)], own_rows)
    last, weight_grad, shaped, outer, early = lax.optimization_barrier(
        (groups[-1][1], weight_grad, shaped, outer, early)
    )
    branch_out = add_parts([(bounds[-1][0], last)], own_rows, early)
    return (branch_out[None], weight_grad[None], *[g[None] for g in shaped], *outer)


def shards(
    queries, keys, values, out_weight, cotangent, local_params, global_params, momentum, frag_index
):
    local_sel = lax.dynamic_index_in_dim(local_params[0], frag_index[0], 0, keepdims=False)

    def finish(summed):
        return outer_update(summed, global_params, momentum, frag_index)

    return inner_step(queries, keys, values, out_weight, cotangent, local_sel, finish)


def solution(mesh):
    placed = (
        P("rep", None, "tp"),
        P("rep", None, "tp"),
        P("rep", None, "tp"),
        P("rep", "tp", None),
        P("rep", "tp", None),
        P("rep", None, "tp", None),
        P(None, "tp", None),
        P(None, "tp", None),
        P(),
    )
    return jax.shard_map(
        shards,
        mesh=mesh,
        in_specs=placed,
        out_specs=(
            P("rep", "tp", None),
            P("rep", "tp", None),
            P("rep", None, "tp"),
            P("rep", None, "tp"),
            P("rep", None, "tp"),
            P("tp", None),
            P("tp", None),
        ),
        check_vma=False,
    )
```

```python
import jax
import jax.numpy as jnp
from jax import lax
from jax.experimental import pallas as pl
from jax.experimental.pallas import tpu as pltpu
from jax.sharding import PartitionSpec as P

HD = 128
LEN = 512
SEQS = 1


outer_momentum = 0.9
outer_rate = 0.7


def nesterov(outer_old, moment_old, summed):
    average = summed / lax.axis_size("rep")
    pseudo_grad = outer_old - average
    new_momentum = outer_momentum * moment_old + pseudo_grad
    new_global = outer_old - outer_rate * (outer_momentum * new_momentum + pseudo_grad)
    return (new_global, new_momentum)


def swap_add(total, step):
    size = lax.axis_size("rep")
    other = lax.ppermute(total, "rep", [(r, r ^ step) for r in range(size)])
    return total.astype(jnp.float32) + other.astype(jnp.float32)


def sum_steps():
    size = lax.axis_size("rep")
    if size & (size - 1):
        raise ValueError("rep")
    return [1 << i for i in range(size.bit_length() - 1)]


def outer_update(summed, global_params, momentum, frag_index):
    chosen = frag_index[0]
    outer_old = lax.dynamic_index_in_dim(global_params, chosen, 0, keepdims=False)
    moment_old = lax.dynamic_index_in_dim(momentum, chosen, 0, keepdims=False)
    return nesterov(outer_old, moment_old, summed)


def sibling_pairs(size):
    return [(t, t ^ 1) for t in range(size)]


def chip_shift(size, step):
    chips = size // 2
    return [(t, ((t // 2 + step) % chips) * 2 + t % 2) for t in range(size)]


def rows_of(array, owner, count):
    return lax.dynamic_slice_in_dim(array, owner * count, count, 0)


def dot(a, b, over):
    return lax.dot_general(a, b, ((over[:1], over[1:]), ((), ())), preferred_element_type=jnp.float32)


def vmem(mib):
    return pltpu.CompilerParams(vmem_limit_bytes=mib * 2**20)


def cost(flops, *arrays):
    moved = sum(a.size * a.dtype.itemsize for a in arrays)
    return pl.CostEstimate(flops=flops, bytes_accessed=moved, transcendentals=0)


def column_block(cols):
    return 1024 if cols % 1024 == 0 else cols


def softmax_rows(query, key, first):
    scores = dot(query, key, (1, 1)) * HD ** (-0.5)
    row = lax.broadcasted_iota(jnp.int32, scores.shape, 0) + first
    col = lax.broadcasted_iota(jnp.int32, scores.shape, 1)
    scores = jnp.where(row >= col, scores, -1e30)
    weights = jnp.exp(scores - jnp.max(scores, axis=-1, keepdims=True))
    return weights / jnp.sum(weights, axis=-1, keepdims=True)


ROWS = 256


def forward_kernel(q_ref, k_ref, v_ref, out_ref):
    for first in range(0, LEN, ROWS):
        end = first + ROWS
        probs = softmax_rows(q_ref[first:end, :], k_ref[:end, :], first)
        out_ref[first:end, :] = dot(probs.astype(jnp.bfloat16), v_ref[:end, :], (1, 0)).astype(
            jnp.bfloat16
        )


def backward_kernel(q_ref, k_ref, v_ref, g_ref, dq_ref, dk_ref, dv_ref, dk_acc, dv_acc):
    dk_acc[...] = jnp.zeros_like(dk_acc)
    dv_acc[...] = jnp.zeros_like(dv_acc)
    for first in range(0, LEN, ROWS):
        end = first + ROWS
        query, grad = q_ref[first:end, :], g_ref[first:end, :]
        probs = softmax_rows(query, k_ref[:end, :], first)
        probs_grad = dot(grad, v_ref[:end, :], (1, 1))
        inner = jnp.sum(probs * probs_grad, axis=-1, keepdims=True)
        score_grad = (probs * (probs_grad - inner) * HD ** (-0.5)).astype(jnp.bfloat16)
        dq_ref[first:end, :] = dot(score_grad, k_ref[:end, :], (1, 0)).astype(jnp.bfloat16)
        dk_acc[:end, :] += dot(score_grad, query, (0, 0))
        dv_acc[:end, :] += dot(probs.astype(jnp.bfloat16), grad, (0, 0))
    dk_ref[...] = dk_acc[...].astype(jnp.bfloat16)
    dv_ref[...] = dv_acc[...].astype(jnp.bfloat16)


def attention_forward(query, key, value):
    spec = pl.BlockSpec((LEN, HD), lambda h: (0, h))
    return pl.pallas_call(
        forward_kernel,
        grid=(query.shape[1] // HD,),
        in_specs=[spec] * 3,
        out_specs=spec,
        out_shape=jax.ShapeDtypeStruct(query.shape, jnp.bfloat16),
        compiler_params=vmem(32),
    )(query, key, value)


def attention_backward(query, key, value, grad):
    spec = pl.BlockSpec((LEN, HD), lambda h: (0, h))
    return pl.pallas_call(
        backward_kernel,
        grid=(query.shape[1] // HD,),
        in_specs=[spec] * 4,
        out_specs=[spec] * 3,
        out_shape=[jax.ShapeDtypeStruct(query.shape, jnp.bfloat16)] * 3,
        scratch_shapes=[pltpu.VMEM((LEN, HD), jnp.float32)] * 2,
        compiler_params=vmem(32),
        cost_estimate=cost(10 * LEN * query.size, query, key, value, grad, query, key, value),
    )(query, key, value, grad)


def branch_kernel(mine_ref, taken_ref, here_ref, near_ref, *out_refs):
    total = dot(mine_ref[...], here_ref[...], (1, 0)) + dot(taken_ref[...], near_ref[...], (1, 0))
    rows = out_refs[0].shape[0]
    for k, out in enumerate(out_refs):
        out[...] = total[k * rows : (k + 1) * rows].astype(out.dtype)


def branch_parts(mine, taken, here, near, chips):
    rows, cols = mine.shape[0] // chips, here.shape[1]
    block = column_block(cols)
    whole = pl.BlockSpec(mine.shape, lambda i: (0, 0))
    weight = pl.BlockSpec((here.shape[0], block), lambda i: (0, i))
    out = jax.ShapeDtypeStruct((rows, cols), jnp.bfloat16)
    return pl.pallas_call(
        branch_kernel,
        grid=(cols // block,),
        in_specs=[whole, whole, weight, weight],
        out_specs=[pl.BlockSpec((rows, block), lambda i: (0, i))] * chips,
        out_shape=[out] * chips,
        compiler_params=vmem(32),
    )(mine, taken, here, near)


def grads_kernel(*refs):
    context_ref, weight_ref, *cot_refs = refs[:-3]
    wgrad_ref, cgrad_ref, total = refs[-3:]
    step = pl.program_id(0)

    @pl.when(step == 0)
    def _():
        total[...] = jnp.zeros_like(total)

    cot = jnp.concatenate([c[...] for c in cot_refs], axis=0)
    wgrad_ref[...] = dot(context_ref[...], cot, (1, 0)).astype(wgrad_ref.dtype)
    total[...] += dot(cot, weight_ref[...], (1, 1))

    @pl.when(step == pl.num_programs(0) - 1)
    def _():
        cgrad_ref[...] = total[...].astype(cgrad_ref.dtype)


def projection_grads(context_t, weight, cots):
    features, tokens = context_t.shape
    rows, cols = cots[0].shape
    block = column_block(cols)
    column = pl.BlockSpec((features, block), lambda i: (0, i))
    out = [
        jax.ShapeDtypeStruct((features, cols), jnp.bfloat16),
        jax.ShapeDtypeStruct((tokens, features), jnp.bfloat16),
    ]
    return pl.pallas_call(
        grads_kernel,
        grid=(cols // block,),
        in_specs=[pl.BlockSpec((features, tokens), lambda i: (0, 0)), column]
        + [pl.BlockSpec((rows, block), lambda i: (0, i))] * len(cots),
        out_specs=[column, pl.BlockSpec((tokens, features), lambda i: (0, 0))],
        out_shape=out,
        scratch_shapes=[pltpu.VMEM((tokens, features), jnp.float32)],
        compiler_params=vmem(32),
        cost_estimate=cost(4 * tokens * features * cols, context_t, weight, *cots, *out),
    )(context_t, weight, *cots)


def inner_step(queries, keys, values, out_weight, cotangent, local_sel, finish):
    weight_here = out_weight[0]
    cot_here = cotangent[0]
    own_rows = cot_here.shape[0]
    size = lax.axis_size("tp")
    chips = size // 2
    me = lax.axis_index("tp")
    chip, core = me // 2, me % 2
    pairs = sibling_pairs(size)

    cot_far = [lax.ppermute(cot_here, "tp", chip_shift(size, k)) for k in range(1, chips)]
    cot_near = lax.ppermute(cot_here, "tp", pairs)
    weight_near = lax.ppermute(weight_here, "tp", pairs)

    context = attention_forward(queries[0], keys[0], values[0])
    summed = local_sel
    for bit in sum_steps()[:1]:
        summed = swap_add(summed, bit)

    give = jnp.concatenate(
        [rows_of(context, ((chip + k) % chips) * 2 + 1 - core, own_rows) for k in range(chips)]
    )
    taken = lax.ppermute(give, "tp", pairs)
    mine = jnp.concatenate(
        [rows_of(context, ((chip + k) % chips) * 2 + core, own_rows) for k in range(chips)]
    )
    own, *far = branch_parts(mine, taken, weight_here, weight_near, chips)
    far, cot_far, own, summed = lax.optimization_barrier((far, cot_far, own, summed))
    got = [lax.ppermute(p, "tp", chip_shift(size, k)) for k, p in enumerate(far, 1)]

    cot_far_near = [lax.ppermute(c, "tp", pairs) for c in cot_far]
    blocks = [cot_here, cot_near]
    owners = [me, chip * 2 + 1 - core]
    for k in range(1, chips):
        from_chip = (chip - k + chips) % chips
        blocks += [cot_far[k - 1], cot_far_near[k - 1]]
        owners += [from_chip * 2 + core, from_chip * 2 + 1 - core]
    context_rows = jnp.concatenate([rows_of(context, o, own_rows) for o in owners])
    weight_grad, part_grad = projection_grads(context_rows.T, weight_here, blocks)
    part_grad, summed = lax.optimization_barrier((part_grad, summed))
    for bit in sum_steps()[1:]:
        summed = swap_add(summed, bit)
    context_grad = jnp.zeros_like(context)
    for i, o in enumerate(owners):
        context_grad = lax.dynamic_update_slice_in_dim(
            context_grad, part_grad[i * own_rows : (i + 1) * own_rows], o * own_rows, 0
        )
    shaped = attention_backward(queries[0], keys[0], values[0], context_grad)
    outer = finish(summed)
    got, weight_grad, shaped, outer = lax.optimization_barrier((got, weight_grad, shaped, outer))
    branch_out = own.astype(jnp.float32)
    for part in got:
        branch_out = branch_out + part.astype(jnp.float32)
    branch_out = branch_out.astype(jnp.bfloat16)
    return (branch_out[None], weight_grad[None], *[g[None] for g in shaped], *outer)


def shards(
    queries, keys, values, out_weight, cotangent, local_params, global_params, momentum, frag_index
):
    local_sel = lax.dynamic_index_in_dim(local_params[0], frag_index[0], 0, keepdims=False)

    def finish(summed):
        return outer_update(summed, global_params, momentum, frag_index)

    return inner_step(queries, keys, values, out_weight, cotangent, local_sel, finish)


def solution(mesh):
    placed = (
        P("rep", None, "tp"),
        P("rep", None, "tp"),
        P("rep", None, "tp"),
        P("rep", "tp", None),
        P("rep", "tp", None),
        P("rep", None, "tp", None),
        P(None, "tp", None),
        P(None, "tp", None),
        P(),
    )
    return jax.shard_map(
        shards,
        mesh=mesh,
        in_specs=placed,
        out_specs=(
            P("rep", "tp", None),
            P("rep", "tp", None),
            P("rep", None, "tp"),
            P("rep", None, "tp"),
            P("rep", None, "tp"),
            P("tp", None),
            P("tp", None),
        ),
        check_vma=False,
    )
```
